256 devices in a mesh: node: 32 (over y_hi, z, core), local: 8 (over x, y_lo).
Axes of the slice: x: 4, y: 4 (y_hi: 2, y_lo: 2; y = y_hi * 2 + y_lo), z: 8, core: 2. Of those that a mesh axis runs over, the one named last changes fastest.
Arguments:
- activations: bfloat16 [2, 81920, 8192], P(None, ('node', 'local')), may hold values from -24 to 24
- cotangent: bfloat16 [2, 81920, 512], P(None, ('node', 'local')), may hold values from -6 to 6
- master: float32 [8192, 512], P('node', 'local'), may hold values from -0.0625 to 0.0625
- first_moment: float32 [8192, 512], P('node', 'local'), may hold values from -3 to 3
- second_moment: float32 [8192, 512], P('node', 'local'), may hold values from 0.05 to 2
Outputs:
- keys: bfloat16 [2, 81920, 512], P(None, ('node', 'local'))
- new_master: float32 [8192, 512], P('node', 'local')
- new_first: float32 [8192, 512], P('node', 'local')
- new_second: float32 [8192, 512], P('node', 'local')
The draws below stay inside these ranges and needn't reach their ends.
All inputs are finite; a program needn't handle non-finite values.
Results may differ from the reference program's by a relative error of at most 0.006.
Values may be sent and summed in bfloat16 or wider, within the bound.
A program may use at most 128 MiB of HBM per device.

```python
import math
import jax
import jax.numpy as jnp
from jax import lax

D = 8192
F = 512
MB = 2
TOK_MB = 320
TOKENS = 81920
N_NODE = 32
N_LOCAL = 8


def strengthened(values, rng, source, target, shards_of, factor):
    owner, partner = [(jnp.arange(values.shape[position]) // (values.shape[position] // shards_of)).reshape([-1 if axis == position else 1 for axis in range(values.ndim)]) for position in (source, target)]
    chosen = jax.random.permutation(rng, shards_of)[partner]
    strong = (owner == chosen) | (owner == (partner + shards_of // 2) % shards_of)
    return jnp.where(strong, factor * values, values)


def block_scale(key, dims, pieces, smallest, top_value):
    def one(position, blocks):
        draws = jax.random.uniform(jax.random.fold_in(jax.random.fold_in(key, 6), position), (blocks,), jnp.float32, smallest / len(pieces), top_value / len(pieces))
        return jnp.repeat(jnp.exp(draws), dims[position] // blocks).reshape((-1,) + (1,) * (len(dims) - position - 1))

    gain = one(*pieces[0])
    for cut in pieces[1:]:
        gain = gain * one(*cut)
    return gain


def normal_values(key, shape, scale, limit, shards=(), held_as=jnp.bfloat16):
    array = scale * jax.random.normal(key, shape, jnp.float32)
    if shards:
        array = array * block_scale(key, shape, shards, -0.22, 0.18)
    return jnp.clip(array, -limit, limit).astype(held_as)


def noise_with(key, extent, deviation, most, split, heavy, held_as=jnp.bfloat16):
    result = deviation * jax.random.normal(key, extent, jnp.float32)
    if split:
        result = result * block_scale(key, extent, split, -0.22, 0.18)
    return jnp.clip(strengthened(result, jax.random.fold_in(key, 3), *heavy), -most, most).astype(held_as)


def setup_inputs(seed: int = 0) -> dict:
    key_of = jax.random.split(jax.random.key(seed), 6)
    return {
        "activations": noise_with(key_of[0], (MB, TOKENS, D), 1.0, 24.0, ((1, 256),), (1, 2, 256, 6.0)),
        "cotangent": normal_values(key_of[1], (MB, TOKENS, F), 1.0, 6.0, ((1, 256),)),
        "master": normal_values(key_of[2], (D, F), D ** -0.5, 0.0625, ((0, 32), (1, 8)), jnp.float32),
        "first_moment": normal_values(key_of[3], (D, F), 0.5, 3.0, ((0, 32), (1, 8)), jnp.float32),
        "second_moment": jnp.clip(jnp.exp(math.log(2.0) - 3.6888794 * jax.random.uniform(key_of[4], (D, F), jnp.float32) ** block_scale(key_of[4], (D, F), ((0, 32), (1, 8)), -0.2, 0.2)), 0.05, 2.0),
    }


def reference(activations, cotangent, master, first_moment, second_moment):
    weight = master.astype(jnp.bfloat16)

    def project(rows):
        return jnp.dot(rows, weight, preferred_element_type=jnp.float32).astype(jnp.bfloat16)
    keys = lax.map(project, activations)
    groups = N_NODE * N_LOCAL
    gscale = 1.0 / math.sqrt(MB * TOKENS)
    acts = activations.reshape(MB, groups, TOK_MB, D)
    cots = cotangent.reshape(MB, groups, TOK_MB, F)

    def add_group(carry, group):
        xs = lax.dynamic_index_in_dim(acts, group, 1, keepdims=False).reshape(MB * TOK_MB, D)
        cs = lax.dynamic_index_in_dim(cots, group, 1, keepdims=False).reshape(MB * TOK_MB, F)
        total = jnp.dot(xs.T, cs, preferred_element_type=jnp.float32)
        term = (total * gscale).astype(jnp.bfloat16)
        return (carry + term.astype(jnp.float32), None)
    grad, _ = lax.scan(add_group, jnp.zeros((D, F), jnp.float32), jnp.arange(groups, dtype=jnp.int32))
    new_first = 0.9 * first_moment + 0.1 * grad
    new_second = 0.95 * second_moment + 0.05 * grad * grad
    mhat = new_first / (1.0 - 0.9 ** 10)
    vhat = new_second / (1.0 - 0.95 ** 10)
    new_master = master - 0.0003 * (mhat / (jnp.sqrt(vhat) + 1e-08) + 0.1 * master)
    return (keys, new_master, new_first, new_second)
```

```python
import functools
import math

import jax
import jax.numpy as jnp
from jax import lax
from jax.experimental import pallas as pl
from jax.experimental.pallas import tpu as pltpu
from jax.sharding import PartitionSpec as P

BF = jnp.bfloat16
F32 = jnp.float32
MESH = pl.DeviceIdType.MESH

RS_B2, RS_C, RS_D = 0, 2, 4
AG_A, AG_B, AG_C, AG_K = 1, 3, 5, 6
P2_AT = 6


def device_of(x, y, z, c):
    return ((y // 2) * 16 + z * 2 + c, x * 2 + y % 2)


def kernel(gscale, a_hbm, c_hbm, w_ref, keys_ref, grad_ref,
           a, cb, ct, wt, g, rsib, r1ax, r1bx, r1ay, r1by, r2x, r2y, r3, acc,
           sem_a, sem_c,
           ag1s, ag1r, ag2s, ag2r, agas, agar, agbs, agbr, agcs, agcr,
           sibs, sibr, rsas, rsar, rsbs, rsbr, rs2s, rs2r, rs3s, rs3r):
    node, local = lax.axis_index("node"), lax.axis_index("local")
    c, z, yh = node % 2, (node // 2) % 8, node // 16
    x, yl = local // 2, local % 2
    y = yh * 2 + yl
    lo, hi = pl.ds(0, 128), pl.ds(128, 128)

    def at_x(d):
        return device_of((x + d) % 4, y, z, c)

    def at_y(d):
        return device_of(x, (y + d) % 4, z, c)

    def at_z(d):
        return device_of(x, y, (z + d) % 8, c)

    sibling = device_of(x, y, z, 1 - c)

    def send(src, dst, ss, rs, device):
        return pltpu.make_async_remote_copy(
            src_ref=src, dst_ref=dst, send_sem=ss, recv_sem=rs, device_id=device, device_id_type=MESH
        )

    def far_first(i):
        return (z + jnp.where(i % 2 == 1, 4 - (i + 1) // 2, 4 + i // 2)) % 8

    def near_first(i):
        return far_first(7 - i)

    barrier = pltpu.get_barrier_semaphore()
    partners = [at_x(d) for d in (1, 2, 3)] + [at_y(d) for d in (1, 2, 3)]
    partners += [at_z(d) for d in range(1, 8)] + [sibling]
    for device in partners:
        pl.semaphore_signal(barrier, inc=1, device_id=device, device_id_type=MESH)

    def load_c(m):
        return pltpu.make_async_copy(c_hbm.at[m], cb.at[pl.ds(320 * m, 320)], sem_c.at[m])

    def load_a(zz, h, m):
        block = h * 8 + zz
        return pltpu.make_async_copy(
            a_hbm.at[m, :, pl.ds(pl.multiple_of(block * 512, 512), 512)],
            a.at[block, pl.ds(320 * m, 320)],
            sem_a.at[block, m],
        )

    for m in range(2):
        load_c(m).start()

    @pl.loop(0, 8)
    def _(i):
        zz = far_first(i)
        for h in range(2):
            for m in range(2):
                load_a(zz, h, m).start()

    wt[yh, z, c, x, yl] = w_ref[...]
    pl.semaphore_wait(barrier, len(partners))

    def ag1(d):
        piece = wt.at[yh, z, c, x, yl]
        return send(piece, piece, ag1s.at[d], ag1r.at[d], at_z(d))

    for d in range(1, 8):
        ag1(d).start()

    def ag2(d):
        left = wt.at[yh, :, c, x, yl, :, lo]
        right = wt.at[yh, :, c, x, yl, :, hi]
        return (
            send(left, left, ag2s.at[0, d], ag2r.at[0, d], at_y(d)),
            send(right, right, ag2s.at[1, d], ag2r.at[1, d], at_x(d)),
        )

    def ag2_start():
        for d in range(1, 8):
            ag1(d).wait_recv()
        for d in (1, 3, 2):
            for copy in ag2(d):
                copy.start()

    def aga(zz):
        left = wt.at[:, zz, c, x, :, :, lo]
        right = wt.at[yh, zz, c, :, yl, :, hi]
        return (
            send(left, left, agas.at[0, zz], agar.at[0, zz], at_x(1)),
            send(left, left, agas.at[1, zz], agar.at[1, zz], at_x(3)),
            send(right, right, agas.at[2, zz], agar.at[2, zz], at_y(1)),
            send(right, right, agas.at[3, zz], agar.at[3, zz], at_y(3)),
        )

    def agb(zz):
        before, after = (x + 3) % 4, (x + 1) % 4
        below, above = (y + 3) % 4, (y + 1) % 4
        parts = (
            wt.at[0, zz, c, before, :, :, lo],
            wt.at[1, zz, c, after, :, :, lo],
            wt.at[below // 2, zz, c, pl.ds(0, 2), below % 2, :, hi],
            wt.at[above // 2, zz, c, pl.ds(2, 2), above % 2, :, hi],
        )
        to = (at_x(1), at_x(3), at_y(1), at_y(3))
        return tuple(
            send(parts[k], parts[k], agbs.at[k, zz], agbr.at[k, zz], to[k]) for k in range(4)
        )

    def agc(zz):
        part = wt.at[:, zz, c]
        return send(part, part, agcs.at[zz], agcr.at[zz], sibling)

    def sib(zz, h):
        return send(
            g.at[h, zz, 1 - c], rsib.at[h, zz], sibs.at[h, zz], sibr.at[h, zz], sibling
        )

    def rs_terms(i):
        zz = far_first(i)
        for h in range(2):
            for m in range(2):
                load_a(zz, h, m).wait()
            for half in range(2):
                total = jnp.dot(
                    ct[256 * half : 256 * half + 256, :], a[h * 8 + zz], preferred_element_type=F32
                )
                term = (total * gscale).astype(BF)
                for q in range(2):
                    g[h, zz, q, 2 * half : 2 * half + 2] = term[:, 256 * q : 256 * q + 256].reshape(
                        2, 2, 64, 256
                    )
            sib(zz, h).start()

    def add(*terms):
        total = terms[0].astype(F32)
        for term in terms[1:]:
            total = total + term.astype(F32)
        return total.astype(BF)

    def rsa(zz):
        far_x = (x + 2) % 4
        return (
            send(g.at[0, zz, c, far_x, :, :, lo], r1ax.at[0, zz], rsas.at[0, zz], rsar.at[0, zz], at_x(1)),
            send(g.at[1, zz, c, far_x, :, :, lo], r1ax.at[1, zz], rsas.at[1, zz], rsar.at[1, zz], at_x(3)),
            send(g.at[1 - yh, zz, c, pl.ds(0, 2), yl, :, hi], r1ay.at[0, zz], rsas.at[2, zz],
                 rsar.at[2, zz], at_y(1)),
            send(g.at[1 - yh, zz, c, pl.ds(2, 2), yl, :, hi], r1ay.at[1, zz], rsas.at[3, zz],
                 rsar.at[3, zz], at_y(3)),
        )

    def rs_pair(i):
        zz = far_first(i)
        for h in range(2):
            sib(zz, h).wait_recv()

            @pl.loop(0, 4)
            def _(k):
                g[h, zz, c, k] = add(g[h, zz, c, k], rsib[h, zz, k])

        for copy in rsa(zz):
            copy.start()

    def rsb(zz):
        before, after = (x + 3) % 4, (x + 1) % 4
        below, above = (y + 3) % 4, (y + 1) % 4
        return (
            send(g.at[:, zz, c, after, :, :, lo], r1bx.at[0, zz], rsbs.at[0, zz], rsbr.at[0, zz], at_x(1)),
            send(g.at[:, zz, c, before, :, :, lo], r1bx.at[1, zz], rsbs.at[1, zz], rsbr.at[1, zz], at_x(3)),
            send(g.at[above // 2, zz, c, :, above % 2, :, hi], r1by.at[0, zz], rsbs.at[2, zz],
                 rsbr.at[2, zz], at_y(1)),
            send(g.at[below // 2, zz, c, :, below % 2, :, hi], r1by.at[1, zz], rsbs.at[3, zz],
                 rsbr.at[3, zz], at_y(3)),
        )

    def rs_pass(i):
        zz = far_first(i)
        before, after = (x + 3) % 4, (x + 1) % 4
        below, above = (y + 3) % 4, (y + 1) % 4
        for copy in rsa(zz):
            copy.wait_recv()
        g[0, zz, c, after, :, :, lo] = add(g[0, zz, c, after, :, :, lo], r1ax[0, zz])
        g[1, zz, c, before, :, :, lo] = add(g[1, zz, c, before, :, :, lo], r1ax[1, zz])
        for k in range(2):
            g[above // 2, zz, c, k, above % 2, :, hi] = add(
                g[above // 2, zz, c, k, above % 2, :, hi], r1ay[0, zz, k]
            )
            g[below // 2, zz, c, 2 + k, below % 2, :, hi] = add(
                g[below // 2, zz, c, 2 + k, below % 2, :, hi], r1ay[1, zz, k]
            )
        for copy in rsb(zz):
            copy.start()

    def rs2(zz, d):
        to_y, to_x = (y + d) % 4, (x + d) % 4
        return (
            send(g.at[to_y // 2, zz, c, x, to_y % 2, :, lo], r2x.at[d - 1, zz], rs2s.at[0, d, zz],
                 rs2r.at[0, d, zz], at_y(d)),
            send(g.at[yh, zz, c, to_x, yl, :, hi], r2y.at[d - 1, zz], rs2s.at[1, d, zz],
                 rs2r.at[1, d, zz], at_x(d)),
        )

    def rs_second(i):
        zz = far_first(i)
        for copy in rsb(zz):
            copy.wait_recv()
        for h in range(2):
            for k in range(2):
                g[h, zz, c, x, k, :, lo] = add(
                    g[h, zz, c, x, k, :, lo], r1bx[0, zz, h, k], r1bx[1, zz, h, k]
                )
        for k in range(4):
            g[yh, zz, c, k, yl, :, hi] = add(g[yh, zz, c, k, yl, :, hi], r1by[0, zz, k], r1by[1, zz, k])
        for d in (1, 3, 2):
            for copy in rs2(zz, d):
                copy.start()

    def rs3(zz, d):
        return send(g.at[yh, zz, c, x, yl], r3.at[d], rs3s.at[d], rs3r.at[d], device_of(x, y, zz, c))

    def rs_third(i):
        zz = far_first(i)
        for d in (1, 2, 3):
            for copy in rs2(zz, d):
                copy.wait_recv()
        g[yh, zz, c, x, yl, :, lo] = add(
            g[yh, zz, c, x, yl, :, lo], r2x[0, zz], r2x[1, zz], r2x[2, zz]
        )
        g[yh, zz, c, x, yl, :, hi] = add(
            g[yh, zz, c, x, yl, :, hi], r2y[0, zz], r2y[1, zz], r2y[2, zz]
        )

        @pl.when(i < 7)
        def _():
            rs3(zz, (zz - z + 8) % 8).start()

    def project(i):
        zz = near_first(i)
        agc(zz).wait_recv()
        for h in range(2):
            piece = jnp.concatenate(
                [wt[h, zz, q].reshape(512, 256) for q in range(2)], axis=1
            )
            acc[...] += lax.dot_general(
                a[h * 8 + zz], piece, (((1,), (1,)), ((), ())), preferred_element_type=F32
            )

    def ag_a(i):
        for copy in aga(near_first(i)):
            copy.start()

    def ag_b(i):
        zz = near_first(i)
        for copy in aga(zz):
            copy.wait_recv()
        for copy in agb(zz):
            copy.start()

    def ag_c(i):
        zz = near_first(i)
        for copy in agb(zz):
            copy.wait_recv()
        agc(zz).start()

    for m in range(2):
        load_c(m).wait()
    ct[...] = cb[...].T

    @pl.loop(0, 9)
    def _(i):
        pl.when(i < 8)(lambda: rs_terms(i))
        pl.when(i >= 1)(lambda: rs_pair(i - 1))
        pl.when(i == P2_AT)(ag2_start)

    acc[...] = jnp.zeros_like(acc)

    stages = (
        (RS_B2, rs_pass), (RS_C, rs_second), (RS_D, rs_third),
        (AG_A, ag_a), (AG_B, ag_b), (AG_C, ag_c), (AG_K, project),
    )

    def ag2_wait():
        for d in range(1, 4):
            for copy in ag2(d):
                copy.wait_recv()

    @pl.loop(0, 8 + max(at for at, _ in stages))
    def _(t):
        pl.when(t == AG_A)(ag2_wait)
        for at, stage in stages:
            @pl.when((t >= at) & (t < at + 8))
            def _(stage=stage, at=at):
                stage(t - at)

    keys_ref[...] = acc[...].astype(BF).reshape(2, 320, 512)

    total = g[yh, z, c, x, yl].astype(F32)
    for d in range(1, 8):
        rs3(z, d).wait_recv()
        total = total + r3[d].astype(F32)
    grad_ref[...] = total

    for d in range(1, 8):
        ag1(d).wait_send()
        rs3(z, d).wait_send()
    for d in range(1, 4):
        for copy in ag2(d):
            copy.wait_send()

    @pl.loop(0, 8)
    def _(zz):
        for copy in (*aga(zz), *agb(zz), agc(zz), sib(zz, 0), sib(zz, 1), *rsa(zz), *rsb(zz),
                     *rs2(zz, 1), *rs2(zz, 2), *rs2(zz, 3)):
            copy.wait_send()


def per_device(activations, cotangent, master, first_moment, second_moment):
    steps, rows, width = activations.shape
    gscale = 1.0 / math.sqrt(steps * rows * lax.axis_size("node") * lax.axis_size("local"))
    piece = master.astype(BF).T
    any_spec = pl.BlockSpec(memory_space=pl.ANY)
    vmem = pl.BlockSpec(memory_space=pltpu.VMEM)
    dma = pltpu.SemaphoreType.DMA
    keys, grad = pl.pallas_call(
        functools.partial(kernel, gscale),
        out_shape=(
            jax.ShapeDtypeStruct((2, 320, 512), BF),
            jax.ShapeDtypeStruct((64, 256), F32),
        ),
        in_specs=[any_spec, any_spec, vmem],
        out_specs=(vmem, vmem),
        scratch_shapes=[
            pltpu.VMEM((16, 640, 512), BF),
            pltpu.VMEM((640, 512), BF),
            pltpu.VMEM((512, 640), BF),
            pltpu.VMEM((2, 8, 2, 4, 2, 64, 256), BF),
            pltpu.VMEM((2, 8, 2, 4, 2, 64, 256), BF),
            pltpu.VMEM((2, 8, 4, 2, 64, 256), BF),
            pltpu.VMEM((2, 8, 2, 64, 128), BF),
            pltpu.VMEM((2, 8, 2, 2, 64, 128), BF),
            pltpu.VMEM((2, 8, 2, 64, 128), BF),
            pltpu.VMEM((2, 8, 4, 64, 128), BF),
            pltpu.VMEM((3, 8, 64, 128), BF),
            pltpu.VMEM((3, 8, 64, 128), BF),
            pltpu.VMEM((8, 64, 256), BF),
            pltpu.VMEM((640, 512), F32),
            dma((16, 2)), dma((2,)),
            dma((8,)), dma((8,)), dma((2, 4)), dma((2, 4)), dma((4, 8)), dma((4, 8)),
            dma((4, 8)), dma((4, 8)), dma((8,)), dma((8,)),
            dma((2, 8)), dma((2, 8)), dma((4, 8)), dma((4, 8)), dma((4, 8)), dma((4, 8)),
            dma((2, 4, 8)), dma((2, 4, 8)), dma((8,)), dma((8,)),
        ],
        compiler_params=pltpu.CompilerParams(
            collective_id=0, has_side_effects=True, vmem_limit_bytes=56 << 20
        ),
        cost_estimate=pl.CostEstimate(
            flops=4 * steps * rows * width * 512, bytes_accessed=12 << 20, transcendentals=0
        ),
        name="project_and_reduce",
    )(activations, cotangent, piece)
    grad = grad.T
    new_first = 0.9 * first_moment + 0.1 * grad
    new_second = 0.95 * second_moment + 0.05 * grad * grad
    mhat = new_first / (1.0 - 0.9**10)
    vhat = new_second / (1.0 - 0.95**10)
    new_master = master - 0.0003 * (mhat / (jnp.sqrt(vhat) + 1e-08) + 0.1 * master)
    return (keys, new_master, new_first, new_second)


def solution(mesh):
    placed = (
        P(None, ("node", "local"), None),
        P(None, ("node", "local"), None),
        P("node", "local"),
        P("node", "local"),
        P("node", "local"),
    )
    return jax.shard_map(
        per_device,
        mesh=mesh,
        in_specs=placed,
        out_specs=(
            P(None, ("node", "local"), None),
            P("node", "local"),
            P("node", "local"),
            P("node", "local"),
        ),
        check_vma=False,
    )
```

```python
import functools
import math

import jax
import jax.numpy as jnp
from jax import lax
from jax.experimental import pallas as pl
from jax.experimental.pallas import tpu as pltpu
from jax.sharding import PartitionSpec as P

BF = jnp.bfloat16
F32 = jnp.float32
MESH = pl.DeviceIdType.MESH

ORDER = "".join((
    "T0T1G1V0G2P0R0G4H0G3P1T2H1G5G6W0B0H2G7R1H4J0P2R2",
    "H3B1T3J1T4H6H5U2P3J2U1T5H7J4T6B2R3P4R4J3P5P6U3U4",
    "T7J6C0J5B3C1P7S0J7S1S2R5S4R6C2B4S3K0U5B6U6B5S5D0",
    "S6K1D1B7C3R7D2C4K2U7C6S7C5K3C7D3K4D4L0D6D5D7",
))

GROUPS = ((0, 1), (2, 3), (4, 5), (6,), (7,))
AHEAD = 2


def device_of(x, y, z, c):
    return ((y // 2) * 16 + z * 2 + c, x * 2 + y % 2)


def kernel(gscale, a_hbm, c_hbm, w_ref, keys_ref, grad_ref,
           a, cb, ct, mb, wt, g, rsib, r1ax, r1bx, r1ay, r1by, r2x, r2y, r3x, r3y, rz, rzb, rz2, rzb2, rz3, rzb3, acc,
           sem_a, sem_c, sem_m,
           ag1s, ag1r, ag2s, ag2r, agas, agar, agbs, agbr, agcs, agcr,
           z1s, z1r, z2s, z2r, zrs, zrr,
           sibs, sibr, rsas, rsar, rsbs, rsbr, rs2s, rs2r, rs3s, rs3r,
           szs, szr, sz2s, sz2r, sz3s, sz3r):
    node, local = lax.axis_index("node"), lax.axis_index("local")
    c, z, yh = node % 2, (node // 2) % 8, node // 16
    x, yl = local // 2, local % 2
    y = yh * 2 + yl
    lo, hi = pl.ds(0, 128), pl.ds(128, 128)
    upper, mid, top, low = pl.ds(0, 32), pl.ds(32, 16), pl.ds(0, 48), pl.ds(48, 16)

    def at_x(d):
        return device_of((x + d) % 4, y, z, c)

    def at_y(d):
        return device_of(x, (y + d) % 4, z, c)

    def at_z(d):
        return device_of(x, y, (z + d) % 8, c)

    sibling = device_of(x, y, z, 1 - c)

    def send(src, dst, ss, rs, device):
        return pltpu.make_async_remote_copy(
            src_ref=src, dst_ref=dst, send_sem=ss, recv_sem=rs, device_id=device, device_id_type=MESH
        )

    def arrived(ref, sem):
        pltpu.make_async_copy(ref, ref, sem).wait()

    def pieces(n):
        for per, rest in (
            (16, ()), (8, (0,)), (6, (0, pl.ds(0, 3))), (4, (0, slice(None), 0)),
            (3, (0, pl.ds(0, 3), 0)), (2, (0, 0)), (1, (0, 0, 0)),
        ):
            if n % per == 0 and n // per <= 8:
                return wt.at[(0, pl.ds(0, n // per), *rest)]

    def far_first(i):
        return (z + (4 - (i + 1) // 2 if i % 2 == 1 else 4 + i // 2)) % 8

    def near_first(i):
        return far_first(7 - i)

    barrier = pltpu.get_barrier_semaphore()
    partners = [at_x(d) for d in (1, 2, 3)] + [at_y(d) for d in (1, 2, 3)]
    partners += [at_z(d) for d in range(1, 8)] + [sibling]
    for device in partners:
        pl.semaphore_signal(barrier, inc=1, device_id=device, device_id_type=MESH)

    def load_c(m):
        return pltpu.make_async_copy(c_hbm.at[m], cb.at[pl.ds(320 * m, 320)], sem_c)

    def load_a(zz, h, m):
        block = h * 8 + zz
        return pltpu.make_async_copy(
            a_hbm.at[m, :, pl.ds(pl.multiple_of(block * 512, 512), 512)],
            a.at[block, pl.ds(320 * m, 320)],
            sem_a.at[zz],
        )

    def load_slice(i):
        zz = far_first(i)
        for h in range(2):
            for m in range(2):
                load_a(zz, h, m).start()

    load_m = pltpu.make_async_copy(w_ref, mb, sem_m)
    load_m.start()
    for m in range(2):
        load_c(m).start()
    for i in range(AHEAD):
        load_slice(i)

    def ag1(d):
        piece = wt.at[yh, z, c, x, yl, top]
        return send(piece, piece, ag1s, ag1r.at[d], at_z(d))

    def agz1(d):
        piece = wt.at[yh, z, c, x, yl, low]
        return send(piece, piece, z1s, z1r, at_y(d))

    def agz2(d):
        piece = wt.at[:, z, c, x, :, low]
        return send(piece, piece, z2s, z2r, at_x(d))

    def ring_send(zz, k, up):
        piece = wt.at[:, zz, c, :, :, low]
        if up:
            return send(piece, piece, zrs, zrr.at[0, k], at_z(1))
        return send(piece, piece, zrs, zrr.at[1, k], at_z(7))

    def ring_half(up):
        if up:
            piece = wt.at[0, (z + 5) % 8, c, :, :, low]
            return send(piece, piece, zrs, zrr.at[0, 4], at_z(1))
        piece = wt.at[1, (z + 3) % 8, c, :, :, low]
        return send(piece, piece, zrs, zrr.at[1, 4], at_z(7))

    def ag2(zz, d):
        left = wt.at[yh, zz, c, x, yl, top, lo]
        right = wt.at[yh, zz, c, x, yl, top, hi]
        return (
            send(left, left, ag2s, ag2r.at[zz], at_y(d)),
            send(right, right, ag2s, ag2r.at[zz], at_x(d)),
        )

    def ag_second(i):
        zz = near_first(i)

        @pl.when(i > 0)
        def _():
            ag1((z - zz + 8) % 8).wait_recv()

        for d in (1, 3, 2):
            for copy in ag2(zz, d):
                copy.start()

    def ag_low_second(_):
        arrived(rz3, z1r)
        for d in (1, 3, 2):
            agz2(d).start()

    def ag_low_third(_):
        arrived(rz2, z2r)
        ring_send(z, 1, True).start()
        ring_send(z, 1, False).start()

    def ag_ring(i):
        k = (i + 1) // 2

        @pl.when((i < 7) & (i % 2 == 1))
        def _():
            ring_send(z, k, True).wait_recv()
            pl.when(k < 3)(lambda: ring_send((z - k + 8) % 8, k + 1, True).start())
            pl.when(k == 3)(lambda: ring_half(True).start())

        @pl.when((i > 0) & (i % 2 == 0))
        def _():
            ring_send(z, k, False).wait_recv()
            pl.when(k < 3)(lambda: ring_send((z + k) % 8, k + 1, False).start())
            pl.when(k == 3)(lambda: ring_half(False).start())

        @pl.when(i == 7)
        def _():
            ring_half(True).wait_recv()
            ring_half(False).wait_recv()

    def aga(zz):
        left = wt.at[:, zz, c, x, :, top, lo]
        right = wt.at[yh, zz, c, :, yl, top, hi]
        return (
            send(left, left, agas, agar.at[zz], at_x(1)),
            send(left, left, agas, agar.at[zz], at_x(3)),
            send(right, right, agas, agar.at[zz], at_y(1)),
            send(right, right, agas, agar.at[zz], at_y(3)),
        )

    def agb(zz):
        before, after = (x + 3) % 4, (x + 1) % 4
        below, above = (y + 3) % 4, (y + 1) % 4
        parts = (
            wt.at[0, zz, c, before, :, top, lo],
            wt.at[1, zz, c, after, :, top, lo],
            wt.at[below // 2, zz, c, pl.ds(0, 2), below % 2, top, hi],
            wt.at[above // 2, zz, c, pl.ds(2, 2), above % 2, top, hi],
        )
        to = (at_x(1), at_x(3), at_y(1), at_y(3))
        return tuple(
            send(parts[k], parts[k], agbs, agbr.at[zz], to[k]) for k in range(4)
        )

    def agc(zz):
        part = wt.at[:, zz, c]
        return send(part, part, agcs, agcr.at[zz], sibling)

    def sib(zz, h):
        return send(
            g.at[h, zz, 1 - c], rsib.at[h, zz], sibs, sibr.at[zz], sibling
        )

    def rs_terms(i):
        zz = far_first(i)
        arrived(a.at[pl.ds(0, 2)], sem_a.at[zz])
        if i + AHEAD < 8:
            load_slice(i + AHEAD)
        rows = jnp.concatenate([a[zz], a[8 + zz]], axis=1)
        for half in range(2):
            total = jnp.dot(
                ct[256 * half : 256 * half + 256, :], rows, preferred_element_type=F32
            )
            term = (total * gscale).astype(BF)
            for h in range(2):
                for q in range(2):
                    col = 512 * h + 256 * q
                    g[h, zz, q, 2 * half : 2 * half + 2] = term[:, col : col + 256].reshape(2, 2, 64, 256)
        for h in range(2):
            sib(zz, h).start()

    def add(*terms):
        total = terms[0].astype(F32)
        for term in terms[1:]:
            total = total + term.astype(F32)
        return total.astype(BF)

    def rsa(zz):
        far_x = (x + 2) % 4
        return (
            send(g.at[0, zz, c, far_x, :, upper, lo], r1ax.at[0, zz], rsas, rsar.at[zz], at_x(1)),
            send(g.at[1, zz, c, far_x, :, upper, lo], r1ax.at[1, zz], rsas, rsar.at[zz], at_x(3)),
            send(g.at[1 - yh, zz, c, pl.ds(0, 2), yl, top, hi], r1ay.at[0, zz], rsas,
                 rsar.at[zz], at_y(1)),
            send(g.at[1 - yh, zz, c, pl.ds(2, 2), yl, top, hi], r1ay.at[1, zz], rsas,
                 rsar.at[zz], at_y(3)),
        )

    def rs_pair(i):
        zz = far_first(i)
        arrived(rsib.at[:, zz], sibr.at[zz])
        for h in range(2):

            @pl.loop(0, 4)
            def _(k):
                g[h, zz, c, k] = add(g[h, zz, c, k], rsib[h, zz, k])

        for copy in rsa(zz):
            copy.start()

    def rsb(zz):
        before, after = (x + 3) % 4, (x + 1) % 4
        below, above = (y + 3) % 4, (y + 1) % 4
        return (
            send(g.at[:, zz, c, after, :, upper, lo], r1bx.at[0, zz], rsbs, rsbr.at[zz], at_x(1)),
            send(g.at[:, zz, c, before, :, upper, lo], r1bx.at[1, zz], rsbs, rsbr.at[zz], at_x(3)),
            send(g.at[above // 2, zz, c, :, above % 2, top, hi], r1by.at[0, zz], rsbs,
                 rsbr.at[zz], at_y(1)),
            send(g.at[below // 2, zz, c, :, below % 2, top, hi], r1by.at[1, zz], rsbs,
                 rsbr.at[zz], at_y(3)),
        )

    def rs_pass(i):
        zz = far_first(i)
        before, after = (x + 3) % 4, (x + 1) % 4
        below, above = (y + 3) % 4, (y + 1) % 4
        arrived(r1ax.at[0, pl.ds(0, 5)], rsar.at[zz])
        g[0, zz, c, after, :, upper, lo] = add(g[0, zz, c, after, :, upper, lo], r1ax[0, zz])
        g[1, zz, c, before, :, upper, lo] = add(g[1, zz, c, before, :, upper, lo], r1ax[1, zz])
        for k in range(2):
            g[above // 2, zz, c, k, above % 2, top, hi] = add(
                g[above // 2, zz, c, k, above % 2, top, hi], r1ay[0, zz, k]
            )
            g[below // 2, zz, c, 2 + k, below % 2, top, hi] = add(
                g[below // 2, zz, c, 2 + k, below % 2, top, hi], r1ay[1, zz, k]
            )
        for copy in rsb(zz):
            copy.start()

    def rs2(zz, d):
        to_y, to_x = (y + d) % 4, (x + d) % 4
        return (
            send(g.at[to_y // 2, zz, c, x, to_y % 2, upper, lo], r2x.at[d - 1, zz], rs2s,
                 rs2r.at[zz], at_y(d)),
            send(g.at[yh, zz, c, to_x, yl, top, hi], r2y.at[d - 1, zz], rs2s,
                 rs2r.at[zz], at_x(d)),
        )

    def rs_second(i):
        zz = far_first(i)
        arrived(r1bx.at[0, pl.ds(0, 5)], rsbr.at[zz])
        for h in range(2):
            for k in range(2):
                g[h, zz, c, x, k, upper, lo] = add(
                    g[h, zz, c, x, k, upper, lo], r1bx[0, zz, h, k], r1bx[1, zz, h, k]
                )
        for k in range(4):
            g[yh, zz, c, k, yl, top, hi] = add(g[yh, zz, c, k, yl, top, hi], r1by[0, zz, k], r1by[1, zz, k])
        for d in (1, 3, 2):
            for copy in rs2(zz, d):
                copy.start()

    def rs3(zz, d):
        own, to = g.at[yh, zz, c, x, yl], device_of(x, y, zz, c)
        return (
            send(own.at[upper, lo], r3x.at[d], rs3s.at[0], rs3r.at[0], to),
            send(own.at[top, hi], r3y.at[d], rs3s.at[1], rs3r.at[1], to),
        )

    def rs_third(i):
        zz = far_first(i)
        arrived(r1by.at[0, pl.ds(0, 5), 0], rs2r.at[zz])
        g[yh, zz, c, x, yl, upper, lo] = add(
            g[yh, zz, c, x, yl, upper, lo], r2x[0, zz], r2x[1, zz], r2x[2, zz]
        )
        g[yh, zz, c, x, yl, top, hi] = add(
            g[yh, zz, c, x, yl, top, hi], r2y[0, zz], r2y[1, zz], r2y[2, zz]
        )

        @pl.when(i < 7)
        def _():
            for copy in rs3(zz, (zz - z + 8) % 8):
                copy.start()

    def rz_send(zz, k, up):
        q = 0 if up else 1
        to = at_z(1) if up else at_z(7)
        return (
            send(g.at[:, zz, c, :, :, low], rz.at[q, k], szs, szr.at[q, k], to),
            send(g.at[:, zz, c, :, :, mid, lo], rzb.at[q, k], szs, szr.at[q, k], to),
        )

    def rz_half(up):
        zz = (z + 4) % 8
        q = 0 if up else 1
        to = at_z(1) if up else at_z(7)
        return (
            send(g.at[q, zz, c, :, :, low], rz.at[q, 4, q], szs, szr.at[q, 4], to),
            send(g.at[q, zz, c, :, :, mid, lo], rzb.at[q, 4, q], szs, szr.at[q, 4], to),
        )

    def start(copies):
        for copy in copies:
            copy.start()

    def rz_arrived(up, k):
        arrived(pieces(3 if k == 4 else 6), szr.at[0 if up else 1, k])

    def rz_add(zz, h, q, k):
        for e in range(4):
            g[h, zz, c, e, :, low] = add(g[h, zz, c, e, :, low], rz[q, k, h, e])
            g[h, zz, c, e, :, mid, lo] = add(g[h, zz, c, e, :, mid, lo], rzb[q, k, h, e])

    def rs_ring(i):
        zz = far_first(i)
        k = 4 - (i + 1) // 2
        j = 4 - i // 2

        @pl.when(i == 0)
        def _():
            start(rz_half(True))
            start(rz_half(False))

        @pl.when((i % 2 == 1) & (i < 7))
        def _():
            @pl.when(k == 3)
            def _():
                rz_arrived(True, 4)
                rz_add(zz, 0, 0, 4)

            @pl.when(k < 3)
            def _():
                rz_arrived(True, k + 1)
                rz_add(zz, 0, 0, k + 1)
                rz_add(zz, 1, 0, k + 1)

            start(rz_send(zz, k, True))

        @pl.when((i % 2 == 0) & (i > 0))
        def _():
            @pl.when(j == 3)
            def _():
                rz_arrived(False, 4)
                rz_add(zz, 1, 1, 4)

            @pl.when(j < 3)
            def _():
                rz_arrived(False, j + 1)
                rz_add(zz, 0, 1, j + 1)
                rz_add(zz, 1, 1, j + 1)

            start(rz_send(zz, j, False))

        @pl.when(i == 7)
        def _():
            for q in range(2):
                rz_arrived(q == 0, 1)
                rz_add(z, 0, q, 1)
                rz_add(z, 1, q, 1)
            for d in (1, 3, 2):
                start(rz_second(d))

    def rz_second(d):
        to_x = (x + d) % 4
        return (
            send(g.at[:, z, c, to_x, :, low], rz2.at[d - 1], sz2s, sz2r, at_x(d)),
            send(g.at[:, z, c, to_x, :, mid, lo], rzb2.at[d - 1], sz2s, sz2r, at_x(d)),
        )

    def rz_third(d):
        to_y = (y + d) % 4
        part = g.at[to_y // 2, z, c, x, to_y % 2]
        return (
            send(part.at[low], rz3.at[d - 1], sz3s, sz3r, at_y(d)),
            send(part.at[mid, lo], rzb3.at[d - 1], sz3s, sz3r, at_y(d)),
        )

    def rz_last(_):
        arrived(r1by.at[0, pl.ds(0, 3)], sz2r)
        for h in range(2):
            for k in range(2):
                g[h, z, c, x, k, low] = add(
                    g[h, z, c, x, k, low], rz2[0, h, k], rz2[1, h, k], rz2[2, h, k]
                )
                g[h, z, c, x, k, mid, lo] = add(
                    g[h, z, c, x, k, mid, lo], rzb2[0, h, k], rzb2[1, h, k], rzb2[2, h, k]
                )
        for d in (1, 3, 2):
            start(rz_third(d))

    def project(group):
        slices = [near_first(i) for i in GROUPS[group]]
        for zz in slices:
            agc(zz).wait_recv()
        blocks = [(h, zz) for zz in slices for h in range(2)]
        rows = jnp.concatenate([a[h * 8 + zz] for h, zz in blocks], axis=1)
        piece = jnp.concatenate(
            [wt[h, zz, q].reshape(512, 256) for h, zz in blocks for q in range(2)], axis=1
        )
        total = lax.dot_general(rows, piece, (((1,), (1,)), ((), ())), preferred_element_type=F32)
        if group > 0:
            total = acc[...] + total
        if group < len(GROUPS) - 1:
            acc[...] = total
        else:
            keys_ref[...] = total.astype(BF).reshape(2, 320, 512)

    def ag_a(i):
        zz = near_first(i)
        arrived(r2y.at[:, pl.ds(0, 2)], ag2r.at[zz])
        for copy in aga(zz):
            copy.start()

    def ag_b(i):
        zz = near_first(i)
        arrived(r1ay.at[0], agar.at[zz])
        for copy in agb(zz):
            copy.start()

    def ag_c(i):
        zz = near_first(i)
        arrived(r1ay.at[0, pl.ds(0, 4)], agbr.at[zz])
        agc(zz).start()

    load_m.wait()
    wt[yh, z, c, x, yl] = mb[...].astype(BF)
    arrived(cb, sem_c)
    ct[...] = cb[...].T
    pl.semaphore_wait(barrier, len(partners))
    for d in (1, 3, 2):
        agz1(d).start()
    for d in (1, 7, 2, 6, 3, 5, 4):
        ag1(d).start()
    ag_second(0)

    stages = dict(
        T=rs_terms, P=rs_pair, R=rs_ring, B=rs_pass, C=rs_second, D=rs_third, L=rz_last,
        G=ag_second, V=ag_low_second, W=ag_low_third, H=ag_a, J=ag_b, U=ag_ring, S=ag_c, K=project,
    )
    for letter, digit in zip(ORDER[::2], ORDER[1::2]):
        stages[letter](int(digit))

    def total(rows, columns, terms):
        value = g[yh, z, c, x, yl, rows, columns].astype(F32)
        for term in terms:
            value = value + term.astype(F32)
        grad_ref[rows, columns] = value

    arrived(r3x.at[pl.ds(1, 7)], rs3r.at[0])
    arrived(r3y.at[pl.ds(1, 7)], rs3r.at[1])
    total(upper, lo, [r3x[d] for d in range(1, 8)])
    total(top, hi, [r3y[d] for d in range(1, 8)])
    arrived(r1by.at[0, 0, pl.ds(0, 3)], sz3r)
    total(low, pl.ds(0, 256), [rz3[k] for k in range(3)])
    total(mid, lo, [rzb3[k] for k in range(3)])

    for ref, sem in (
        (r1by.at[0, pl.ds(0, 7), pl.ds(0, 2)], ag1s), (rz3, z1s), (rz2, z2s), (pieces(28), zrs),
        (pieces(18), ag2s), (pieces(48), agas), (pieces(24), agbs), (rsib, agcs),
        (rsib, sibs), (pieces(20), rsas), (pieces(40), rsbs), (pieces(15), rs2s),
        (r3x.at[pl.ds(1, 7)], rs3s.at[0]), (r3y.at[pl.ds(1, 7)], rs3s.at[1]), (pieces(42), szs),
        (r1by.at[0, pl.ds(0, 3)], sz2s), (r1by.at[0, 0, pl.ds(0, 3)], sz3s),
    ):
        arrived(ref, sem)


def update(keys_ref, grad_ref, master_ref, first_ref, second_ref,
           keys_out, master_out, first_out, second_out):
    keys_out[...] = keys_ref[...]
    grad, master = grad_ref[...], master_ref[...]
    new_first = 0.9 * first_ref[...] + 0.1 * grad
    new_second = 0.95 * second_ref[...] + 0.05 * grad * grad
    mhat = new_first / (1.0 - 0.9**10)
    vhat = new_second / (1.0 - 0.95**10)
    first_out[...] = new_first
    second_out[...] = new_second
    master_out[...] = master - 0.0003 * (mhat / (jnp.sqrt(vhat) + 1e-08) + 0.1 * master)


def per_device(activations, cotangent, master, first_moment, second_moment):
    steps, rows, width = activations.shape
    gscale = 1.0 / math.sqrt(steps * rows * lax.axis_size("node") * lax.axis_size("local"))
    any_spec = pl.BlockSpec(memory_space=pl.ANY)
    vmem = pl.BlockSpec(memory_space=pltpu.VMEM)
    dma = pltpu.SemaphoreType.DMA
    keys, grad = pl.pallas_call(
        functools.partial(kernel, gscale),
        out_shape=(
            jax.ShapeDtypeStruct((2, 320, 512), BF),
            jax.ShapeDtypeStruct((64, 256), F32),
        ),
        in_specs=[any_spec, any_spec, any_spec],
        out_specs=(vmem, vmem),
        scratch_shapes=[
            pltpu.VMEM((16, 640, 512), BF),
            pltpu.VMEM((640, 512), BF),
            pltpu.VMEM((512, 640), BF),
            pltpu.VMEM((64, 256), F32),
            pltpu.VMEM((2, 8, 2, 4, 2, 64, 256), BF),
            pltpu.VMEM((2, 8, 2, 4, 2, 64, 256), BF),
            pltpu.VMEM((2, 8, 4, 2, 64, 256), BF),
            pltpu.VMEM((2, 8, 2, 32, 128), BF),
            pltpu.VMEM((2, 8, 2, 2, 32, 128), BF),
            pltpu.VMEM((2, 8, 2, 48, 128), BF),
            pltpu.VMEM((2, 8, 4, 48, 128), BF),
            pltpu.VMEM((3, 8, 32, 128), BF),
            pltpu.VMEM((3, 8, 48, 128), BF),
            pltpu.VMEM((8, 32, 128), BF),
            pltpu.VMEM((8, 48, 128), BF),
            pltpu.VMEM((2, 5, 2, 4, 2, 16, 256), BF),
            pltpu.VMEM((2, 5, 2, 4, 2, 16, 128), BF),
            pltpu.VMEM((3, 2, 2, 16, 256), BF),
            pltpu.VMEM((3, 2, 2, 16, 128), BF),
            pltpu.VMEM((3, 16, 256), BF),
            pltpu.VMEM((3, 16, 128), BF),
            pltpu.VMEM((640, 512), F32),
            dma((8,)), dma, dma,
            dma, dma((8,)), dma, dma((8,)), dma, dma((8,)),
            dma, dma((8,)), dma, dma((8,)),
            dma, dma, dma, dma, dma, dma((2, 5)),
            dma, dma((8,)), dma, dma((8,)), dma, dma((8,)),
            dma, dma((8,)), dma((2,)), dma((2,)),
            dma, dma((2, 5)), dma, dma, dma, dma,
        ],
        compiler_params=pltpu.CompilerParams(
            collective_id=0, has_side_effects=True, vmem_limit_bytes=56 << 20
        ),
        cost_estimate=pl.CostEstimate(
            flops=4 * steps * rows * width * 512, bytes_accessed=12 << 20, transcendentals=0
        ),
        name="project_and_reduce",
    )(activations, cotangent, master.T)
    keys, new_master, new_first, new_second = pl.pallas_call(
        update,
        out_shape=(jax.ShapeDtypeStruct((2, 320, 512), BF),) + (jax.ShapeDtypeStruct((64, 256), F32),) * 3,
        in_specs=[vmem] * 5,
        out_specs=(vmem,) * 4,
        name="adam_update",
    )(keys, grad, master.T, first_moment.T, second_moment.T)
    return (keys, new_master.T, new_first.T, new_second.T)


def solution(mesh):
    placed = (
        P(None, ("node", "local"), None),
        P(None, ("node", "local"), None),
        P("node", "local"),
        P("node", "local"),
        P("node", "local"),
    )
    return jax.shard_map(
        per_device,
        mesh=mesh,
        in_specs=placed,
        out_specs=(
            P(None, ("node", "local"), None),
            P("node", "local"),
            P("node", "local"),
            P("node", "local"),
        ),
        check_vma=False,
    )
```

```python
import functools
import math

import jax
import jax.numpy as jnp
from jax import lax
from jax.experimental import pallas as pl
from jax.experimental.pallas import tpu as pltpu
from jax.sharding import PartitionSpec as P

BF = jnp.bfloat16
F32 = jnp.float32
MESH = pl.DeviceIdType.MESH

ORDER = "".join((
    "T0T1G1V0G2P0R0G4H0G3P1T2H1G5G6W0B0H2G7R1H4J0P2R2",
    "H3B1T3J1T4H6H5U2P3J2U1T5H7J4T6B2R3P4R4J3P5P6U3U4",
    "T7J6C0J5B3C1P7S0J7S1S2R5S4R6C2B4S3K0U5B6U6B5S5D0",
    "S6K1D1B7C3R7D2C4K2U7C6S7C5K3C7X0D3Y0D4L0D6D5D7",
))

GROUPS = ((0, 1), (2, 3), (4, 5), (6,))
AHEAD = 2


def device_of(x, y, z, c):
    return ((y // 2) * 16 + z * 2 + c, x * 2 + y % 2)


def kernel(gscale, a_hbm, c_hbm, w_ref, keys_ref, grad_ref,
           a, cb, ct, mb, wt, g, rsib, r1ax, r1bx, r1ay, r1by, r2x, r2y, r3x, r3y, rz, rzb, rz2, rzb2, rz3, rzb3, acc,
           keys, sem_a, sem_c, sem_m, sem_k,
           ag1s, ag1r, ag2s, ag2r, agas, agar, agbs, agbr, agcs, agcr,
           z1s, z1r, z2s, z2r, zrs, zrr,
           sibs, sibr, rsas, rsar, rsbs, rsbr, rs2s, rs2r, rs3s, rs3r,
           szs, szr, sz2s, sz2r, sz3s, sz3r):
    node, local = lax.axis_index("node"), lax.axis_index("local")
    c, z, yh = node % 2, (node // 2) % 8, node // 16
    x, yl = local // 2, local % 2
    y = yh * 2 + yl
    lo, hi = pl.ds(0, 128), pl.ds(128, 128)
    upper, mid, top, low = pl.ds(0, 32), pl.ds(32, 16), pl.ds(0, 48), pl.ds(48, 16)

    def at_x(d):
        return device_of((x + d) % 4, y, z, c)

    def at_y(d):
        return device_of(x, (y + d) % 4, z, c)

    def at_z(d):
        return device_of(x, y, (z + d) % 8, c)

    sibling = device_of(x, y, z, 1 - c)

    def send(src, dst, ss, rs, device):
        return pltpu.make_async_remote_copy(
            src_ref=src, dst_ref=dst, send_sem=ss, recv_sem=rs, device_id=device, device_id_type=MESH
        )

    def arrived(ref, sem):
        pltpu.make_async_copy(ref, ref, sem).wait()

    def pieces(n):
        for per, rest in (
            (16, ()), (8, (0,)), (6, (0, pl.ds(0, 3))), (4, (0, slice(None), 0)),
            (3, (0, pl.ds(0, 3), 0)), (2, (0, 0)), (1, (0, 0, 0)),
        ):
            if n % per == 0 and n // per <= 8:
                return wt.at[(0, pl.ds(0, n // per), *rest)]

    def far_first(i):
        return (z + (4 - (i + 1) // 2 if i % 2 == 1 else 4 + i // 2)) % 8

    def near_first(i):
        return far_first(7 - i)

    barrier = pltpu.get_barrier_semaphore()
    partners = [at_x(d) for d in (1, 2, 3)] + [at_y(d) for d in (1, 2, 3)]
    partners += [at_z(d) for d in range(1, 8)] + [sibling]
    for device in partners:
        pl.semaphore_signal(barrier, inc=1, device_id=device, device_id_type=MESH)

    def load_c(m):
        return pltpu.make_async_copy(c_hbm.at[m], cb.at[pl.ds(320 * m, 320)], sem_c)

    def load_a(zz, h, m):
        block = h * 8 + zz
        return pltpu.make_async_copy(
            a_hbm.at[m, :, pl.ds(pl.multiple_of(block * 512, 512), 512)],
            a.at[block, pl.ds(320 * m, 320)],
            sem_a.at[zz],
        )

    def load_slice(i):
        zz = far_first(i)
        for h in range(2):
            for m in range(2):
                load_a(zz, h, m).start()

    load_m = pltpu.make_async_copy(w_ref, mb, sem_m)
    load_m.start()
    for m in range(2):
        load_c(m).start()
    for i in range(AHEAD):
        load_slice(i)

    def ag1(d):
        piece = wt.at[yh, z, c, x, yl, top]
        return send(piece, piece, ag1s, ag1r.at[d], at_z(d))

    def agz1(d):
        piece = wt.at[yh, z, c, x, yl, low]
        return send(piece, piece, z1s, z1r, at_y(d))

    def agz2(d):
        piece = wt.at[:, z, c, x, :, low]
        return send(piece, piece, z2s, z2r, at_x(d))

    def ring_send(zz, k, up):
        piece = wt.at[:, zz, c, :, :, low]
        if up:
            return send(piece, piece, zrs, zrr.at[0, k], at_z(1))
        return send(piece, piece, zrs, zrr.at[1, k], at_z(7))

    def ring_half(up):
        if up:
            piece = wt.at[0, (z + 5) % 8, c, :, :, low]
            return send(piece, piece, zrs, zrr.at[0, 4], at_z(1))
        piece = wt.at[1, (z + 3) % 8, c, :, :, low]
        return send(piece, piece, zrs, zrr.at[1, 4], at_z(7))

    def ag2(zz, d):
        left = wt.at[yh, zz, c, x, yl, top, lo]
        right = wt.at[yh, zz, c, x, yl, top, hi]
        return (
            send(left, left, ag2s, ag2r.at[zz], at_y(d)),
            send(right, right, ag2s, ag2r.at[zz], at_x(d)),
        )

    def ag_second(i):
        zz = near_first(i)

        @pl.when(i > 0)
        def _():
            ag1((z - zz + 8) % 8).wait_recv()

        for d in (1, 3, 2):
            for copy in ag2(zz, d):
                copy.start()

    def ag_low_second(_):
        arrived(rz3, z1r)
        for d in (1, 3, 2):
            agz2(d).start()

    def ag_low_third(_):
        arrived(rz2, z2r)
        ring_send(z, 1, True).start()
        ring_send(z, 1, False).start()

    def ag_ring(i):
        k = (i + 1) // 2

        @pl.when((i < 7) & (i % 2 == 1))
        def _():
            ring_send(z, k, True).wait_recv()
            pl.when(k < 3)(lambda: ring_send((z - k + 8) % 8, k + 1, True).start())
            pl.when(k == 3)(lambda: ring_half(True).start())

        @pl.when((i > 0) & (i % 2 == 0))
        def _():
            ring_send(z, k, False).wait_recv()
            pl.when(k < 3)(lambda: ring_send((z + k) % 8, k + 1, False).start())
            pl.when(k == 3)(lambda: ring_half(False).start())

        @pl.when(i == 7)
        def _():
            ring_half(True).wait_recv()
            ring_half(False).wait_recv()

    def aga(zz):
        left = wt.at[:, zz, c, x, :, top, lo]
        right = wt.at[yh, zz, c, :, yl, top, hi]
        return (
            send(left, left, agas, agar.at[zz], at_x(1)),
            send(left, left, agas, agar.at[zz], at_x(3)),
            send(right, right, agas, agar.at[zz], at_y(1)),
            send(right, right, agas, agar.at[zz], at_y(3)),
        )

    def agb(zz):
        before, after = (x + 3) % 4, (x + 1) % 4
        below, above = (y + 3) % 4, (y + 1) % 4
        parts = (
            wt.at[0, zz, c, before, :, top, lo],
            wt.at[1, zz, c, after, :, top, lo],
            wt.at[below // 2, zz, c, pl.ds(0, 2), below % 2, top, hi],
            wt.at[above // 2, zz, c, pl.ds(2, 2), above % 2, top, hi],
        )
        to = (at_x(1), at_x(3), at_y(1), at_y(3))
        return tuple(
            send(parts[k], parts[k], agbs, agbr.at[zz], to[k]) for k in range(4)
        )

    def agc(zz):
        part = wt.at[:, zz, c]
        return send(part, part, agcs, agcr.at[zz], sibling)

    def sib(zz, h):
        return send(
            g.at[h, zz, 1 - c], rsib.at[h, zz], sibs, sibr.at[zz], sibling
        )

    def rs_terms(i):
        zz = far_first(i)
        arrived(a.at[pl.ds(0, 2)], sem_a.at[zz])
        if i + AHEAD < 8:
            load_slice(i + AHEAD)
        rows = jnp.concatenate([a[zz], a[8 + zz]], axis=1)
        for half in range(2):
            total = jnp.dot(
                ct[256 * half : 256 * half + 256, :], rows, preferred_element_type=F32
            )
            term = (total * gscale).astype(BF)
            for h in range(2):
                for q in range(2):
                    col = 512 * h + 256 * q
                    g[h, zz, q, 2 * half : 2 * half + 2] = term[:, col : col + 256].reshape(2, 2, 64, 256)
        for h in range(2):
            sib(zz, h).start()

    def add(*terms):
        total = terms[0].astype(F32)
        for term in terms[1:]:
            total = total + term.astype(F32)
        return total.astype(BF)

    def rsa(zz):
        far_x = (x + 2) % 4
        return (
            send(g.at[0, zz, c, far_x, :, upper, lo], r1ax.at[0, zz], rsas, rsar.at[zz], at_x(1)),
            send(g.at[1, zz, c, far_x, :, upper, lo], r1ax.at[1, zz], rsas, rsar.at[zz], at_x(3)),
            send(g.at[1 - yh, zz, c, pl.ds(0, 2), yl, top, hi], r1ay.at[0, zz], rsas,
                 rsar.at[zz], at_y(1)),
            send(g.at[1 - yh, zz, c, pl.ds(2, 2), yl, top, hi], r1ay.at[1, zz], rsas,
                 rsar.at[zz], at_y(3)),
        )

    def rs_pair(i):
        zz = far_first(i)
        arrived(rsib.at[:, zz], sibr.at[zz])
        for h in range(2):

            @pl.loop(0, 4)
            def _(k):
                g[h, zz, c, k] = add(g[h, zz, c, k], rsib[h, zz, k])

        for copy in rsa(zz):
            copy.start()

    def rsb(zz):
        before, after = (x + 3) % 4, (x + 1) % 4
        below, above = (y + 3) % 4, (y + 1) % 4
        return (
            send(g.at[:, zz, c, after, :, upper, lo], r1bx.at[0, zz], rsbs, rsbr.at[zz], at_x(1)),
            send(g.at[:, zz, c, before, :, upper, lo], r1bx.at[1, zz], rsbs, rsbr.at[zz], at_x(3)),
            send(g.at[above // 2, zz, c, :, above % 2, top, hi], r1by.at[0, zz], rsbs,
                 rsbr.at[zz], at_y(1)),
            send(g.at[below // 2, zz, c, :, below % 2, top, hi], r1by.at[1, zz], rsbs,
                 rsbr.at[zz], at_y(3)),
        )

    def rs_pass(i):
        zz = far_first(i)
        before, after = (x + 3) % 4, (x + 1) % 4
        below, above = (y + 3) % 4, (y + 1) % 4
        arrived(r1ax.at[0, pl.ds(0, 5)], rsar.at[zz])
        g[0, zz, c, after, :, upper, lo] = add(g[0, zz, c, after, :, upper, lo], r1ax[0, zz])
        g[1, zz, c, before, :, upper, lo] = add(g[1, zz, c, before, :, upper, lo], r1ax[1, zz])
        for k in range(2):
            g[above // 2, zz, c, k, above % 2, top, hi] = add(
                g[above // 2, zz, c, k, above % 2, top, hi], r1ay[0, zz, k]
            )
            g[below // 2, zz, c, 2 + k, below % 2, top, hi] = add(
                g[below // 2, zz, c, 2 + k, below % 2, top, hi], r1ay[1, zz, k]
            )
        for copy in rsb(zz):
            copy.start()

    def rs2(zz, d):
        to_y, to_x = (y + d) % 4, (x + d) % 4
        return (
            send(g.at[to_y // 2, zz, c, x, to_y % 2, upper, lo], r2x.at[d - 1, zz], rs2s,
                 rs2r.at[zz], at_y(d)),
            send(g.at[yh, zz, c, to_x, yl, top, hi], r2y.at[d - 1, zz], rs2s,
                 rs2r.at[zz], at_x(d)),
        )

    def rs_second(i):
        zz = far_first(i)
        arrived(r1bx.at[0, pl.ds(0, 5)], rsbr.at[zz])
        for h in range(2):
            for k in range(2):
                g[h, zz, c, x, k, upper, lo] = add(
                    g[h, zz, c, x, k, upper, lo], r1bx[0, zz, h, k], r1bx[1, zz, h, k]
                )
        for k in range(4):
            g[yh, zz, c, k, yl, top, hi] = add(g[yh, zz, c, k, yl, top, hi], r1by[0, zz, k], r1by[1, zz, k])
        for d in (1, 3, 2):
            for copy in rs2(zz, d):
                copy.start()

    def rs3(zz, d):
        own, to = g.at[yh, zz, c, x, yl], device_of(x, y, zz, c)
        return (
            send(own.at[upper, lo], r3x.at[d], rs3s.at[0], rs3r.at[0], to),
            send(own.at[top, hi], r3y.at[d], rs3s.at[1], rs3r.at[1], to),
        )

    def rs_third(i):
        zz = far_first(i)
        arrived(r1by.at[0, pl.ds(0, 5), 0], rs2r.at[zz])
        g[yh, zz, c, x, yl, upper, lo] = add(
            g[yh, zz, c, x, yl, upper, lo], r2x[0, zz], r2x[1, zz], r2x[2, zz]
        )
        g[yh, zz, c, x, yl, top, hi] = add(
            g[yh, zz, c, x, yl, top, hi], r2y[0, zz], r2y[1, zz], r2y[2, zz]
        )

        @pl.when(i < 7)
        def _():
            for copy in rs3(zz, (zz - z + 8) % 8):
                copy.start()

    def rz_send(zz, k, up):
        q = 0 if up else 1
        to = at_z(1) if up else at_z(7)
        return (
            send(g.at[:, zz, c, :, :, low], rz.at[q, k], szs, szr.at[q, k], to),
            send(g.at[:, zz, c, :, :, mid, lo], rzb.at[q, k], szs, szr.at[q, k], to),
        )

    def rz_half(up):
        zz = (z + 4) % 8
        q = 0 if up else 1
        to = at_z(1) if up else at_z(7)
        return (
            send(g.at[q, zz, c, :, :, low], rz.at[q, 4, q], szs, szr.at[q, 4], to),
            send(g.at[q, zz, c, :, :, mid, lo], rzb.at[q, 4, q], szs, szr.at[q, 4], to),
        )

    def start(copies):
        for copy in copies:
            copy.start()

    def rz_arrived(up, k):
        arrived(pieces(3 if k == 4 else 6), szr.at[0 if up else 1, k])

    def rz_add(zz, h, q, k):
        for e in range(4):
            g[h, zz, c, e, :, low] = add(g[h, zz, c, e, :, low], rz[q, k, h, e])
            g[h, zz, c, e, :, mid, lo] = add(g[h, zz, c, e, :, mid, lo], rzb[q, k, h, e])

    def rs_ring(i):
        zz = far_first(i)
        k = 4 - (i + 1) // 2
        j = 4 - i // 2

        @pl.when(i == 0)
        def _():
            start(rz_half(True))
            start(rz_half(False))

        @pl.when((i % 2 == 1) & (i < 7))
        def _():
            @pl.when(k == 3)
            def _():
                rz_arrived(True, 4)
                rz_add(zz, 0, 0, 4)

            @pl.when(k < 3)
            def _():
                rz_arrived(True, k + 1)
                rz_add(zz, 0, 0, k + 1)
                rz_add(zz, 1, 0, k + 1)

            start(rz_send(zz, k, True))

        @pl.when((i % 2 == 0) & (i > 0))
        def _():
            @pl.when(j == 3)
            def _():
                rz_arrived(False, 4)
                rz_add(zz, 1, 1, 4)

            @pl.when(j < 3)
            def _():
                rz_arrived(False, j + 1)
                rz_add(zz, 0, 1, j + 1)
                rz_add(zz, 1, 1, j + 1)

            start(rz_send(zz, j, False))

        @pl.when(i == 7)
        def _():
            for q in range(2):
                rz_arrived(q == 0, 1)
                rz_add(z, 0, q, 1)
                rz_add(z, 1, q, 1)
            for d in (1, 3, 2):
                start(rz_second(d))

    def rz_second(d):
        to_x = (x + d) % 4
        return (
            send(g.at[:, z, c, to_x, :, low], rz2.at[d - 1], sz2s, sz2r, at_x(d)),
            send(g.at[:, z, c, to_x, :, mid, lo], rzb2.at[d - 1], sz2s, sz2r, at_x(d)),
        )

    def rz_third(d):
        to_y = (y + d) % 4
        part = g.at[to_y // 2, z, c, x, to_y % 2]
        return (
            send(part.at[low], rz3.at[d - 1], sz3s, sz3r, at_y(d)),
            send(part.at[mid, lo], rzb3.at[d - 1], sz3s, sz3r, at_y(d)),
        )

    def rz_last(_):
        arrived(r1by.at[0, pl.ds(0, 3)], sz2r)
        for h in range(2):
            for k in range(2):
                g[h, z, c, x, k, low] = add(
                    g[h, z, c, x, k, low], rz2[0, h, k], rz2[1, h, k], rz2[2, h, k]
                )
                g[h, z, c, x, k, mid, lo] = add(
                    g[h, z, c, x, k, mid, lo], rzb2[0, h, k], rzb2[1, h, k], rzb2[2, h, k]
                )
        for d in (1, 3, 2):
            start(rz_third(d))

    def project(group):
        slices = [near_first(i) for i in GROUPS[group]]
        for zz in slices:
            agc(zz).wait_recv()
        blocks = [(h, zz) for zz in slices for h in range(2)]
        rows = jnp.concatenate([a[h * 8 + zz] for h, zz in blocks], axis=1)
        piece = jnp.concatenate(
            [wt[h, zz, q].reshape(512, 256) for h, zz in blocks for q in range(2)], axis=1
        )
        total = lax.dot_general(rows, piece, (((1,), (1,)), ((), ())), preferred_element_type=F32)
        acc[...] = acc[...] + total if group > 0 else total

    def project_last(core):
        zz = near_first(7)
        columns = pl.ds(pl.multiple_of(core * 256, 256), 256)
        rows = jnp.concatenate([a[zz, :, columns], a[8 + zz, :, columns]], axis=1)
        piece = jnp.concatenate([wt[h, zz, core].reshape(512, 256) for h in range(2)], axis=1)
        return acc[...] + lax.dot_general(
            rows, piece, (((1,), (1,)), ((), ())), preferred_element_type=F32
        )

    def project_own(_):
        acc[...] = project_last(c)

    def store_keys():
        return pltpu.make_async_copy(keys, keys_ref, sem_k)

    def project_sibling(_):
        agc(near_first(7)).wait_recv()
        keys[...] = project_last(1 - c).astype(BF).reshape(2, 320, 512)
        store_keys().start()

    def ag_a(i):
        zz = near_first(i)
        arrived(r2y.at[:, pl.ds(0, 2)], ag2r.at[zz])
        for copy in aga(zz):
            copy.start()

    def ag_b(i):
        zz = near_first(i)
        arrived(r1ay.at[0], agar.at[zz])
        for copy in agb(zz):
            copy.start()

    def ag_c(i):
        zz = near_first(i)
        arrived(r1ay.at[0, pl.ds(0, 4)], agbr.at[zz])
        agc(zz).start()

    load_m.wait()
    wt[yh, z, c, x, yl] = mb[...].astype(BF)
    arrived(cb, sem_c)
    ct[...] = cb[...].T
    pl.semaphore_wait(barrier, len(partners))
    for d in (1, 3, 2):
        agz1(d).start()
    for d in (1, 7, 2, 6, 3, 5, 4):
        ag1(d).start()
    ag_second(0)

    stages = dict(
        T=rs_terms, P=rs_pair, R=rs_ring, B=rs_pass, C=rs_second, D=rs_third, L=rz_last,
        G=ag_second, V=ag_low_second, W=ag_low_third, H=ag_a, J=ag_b, U=ag_ring, S=ag_c, K=project, X=project_own, Y=project_sibling,
    )
    for letter, digit in zip(ORDER[::2], ORDER[1::2]):
        stages[letter](int(digit))

    def total(rows, columns, terms):
        value = g[yh, z, c, x, yl, rows, columns].astype(F32)
        for term in terms:
            value = value + term.astype(F32)
        grad_ref[rows, columns] = value

    arrived(r3x.at[pl.ds(1, 7)], rs3r.at[0])
    arrived(r3y.at[pl.ds(1, 7)], rs3r.at[1])
    total(upper, lo, [r3x[d] for d in range(1, 8)])
    total(top, hi, [r3y[d] for d in range(1, 8)])
    arrived(r1by.at[0, 0, pl.ds(0, 3)], sz3r)
    total(low, pl.ds(0, 256), [rz3[k] for k in range(3)])
    total(mid, lo, [rzb3[k] for k in range(3)])

    store_keys().wait()

    for ref, sem in (
        (r1by.at[0, pl.ds(0, 7), pl.ds(0, 2)], ag1s), (rz3, z1s), (rz2, z2s), (pieces(28), zrs),
        (pieces(18), ag2s), (pieces(48), agas), (pieces(24), agbs), (rsib, agcs),
        (rsib, sibs), (pieces(20), rsas), (pieces(40), rsbs), (pieces(15), rs2s),
        (r3x.at[pl.ds(1, 7)], rs3s.at[0]), (r3y.at[pl.ds(1, 7)], rs3s.at[1]), (pieces(42), szs),
        (r1by.at[0, pl.ds(0, 3)], sz2s), (r1by.at[0, 0, pl.ds(0, 3)], sz3s),
    ):
        arrived(ref, sem)


def update(keys_ref, grad_ref, master_ref, first_ref, second_ref,
           keys_out, master_out, first_out, second_out):
    keys_out[...] = keys_ref[...]
    grad, master = grad_ref[...], master_ref[...]
    new_first = 0.9 * first_ref[...] + 0.1 * grad
    new_second = 0.95 * second_ref[...] + 0.05 * grad * grad
    mhat = new_first / (1.0 - 0.9**10)
    vhat = new_second / (1.0 - 0.95**10)
    first_out[...] = new_first
    second_out[...] = new_second
    master_out[...] = master - 0.0003 * (mhat / (jnp.sqrt(vhat) + 1e-08) + 0.1 * master)


def per_device(activations, cotangent, master, first_moment, second_moment):
    steps, rows, width = activations.shape
    gscale = 1.0 / math.sqrt(steps * rows * lax.axis_size("node") * lax.axis_size("local"))
    any_spec = pl.BlockSpec(memory_space=pl.ANY)
    vmem = pl.BlockSpec(memory_space=pltpu.VMEM)
    dma = pltpu.SemaphoreType.DMA
    keys, grad = pl.pallas_call(
        functools.partial(kernel, gscale),
        out_shape=(
            jax.ShapeDtypeStruct((2, 320, 512), BF),
            jax.ShapeDtypeStruct((64, 256), F32),
        ),
        in_specs=[any_spec, any_spec, any_spec],
        out_specs=(any_spec, vmem),
        scratch_shapes=[
            pltpu.VMEM((16, 640, 512), BF),
            pltpu.VMEM((640, 512), BF),
            pltpu.VMEM((512, 640), BF),
            pltpu.VMEM((64, 256), F32),
            pltpu.VMEM((2, 8, 2, 4, 2, 64, 256), BF),
            pltpu.VMEM((2, 8, 2, 4, 2, 64, 256), BF),
            pltpu.VMEM((2, 8, 4, 2, 64, 256), BF),
            pltpu.VMEM((2, 8, 2, 32, 128), BF),
            pltpu.VMEM((2, 8, 2, 2, 32, 128), BF),
            pltpu.VMEM((2, 8, 2, 48, 128), BF),
            pltpu.VMEM((2, 8, 4, 48, 128), BF),
            pltpu.VMEM((3, 8, 32, 128), BF),
            pltpu.VMEM((3, 8, 48, 128), BF),
            pltpu.VMEM((8, 32, 128), BF),
            pltpu.VMEM((8, 48, 128), BF),
            pltpu.VMEM((2, 5, 2, 4, 2, 16, 256), BF),
            pltpu.VMEM((2, 5, 2, 4, 2, 16, 128), BF),
            pltpu.VMEM((3, 2, 2, 16, 256), BF),
            pltpu.VMEM((3, 2, 2, 16, 128), BF),
            pltpu.VMEM((3, 16, 256), BF),
            pltpu.VMEM((3, 16, 128), BF),
            pltpu.VMEM((640, 512), F32),
            pltpu.VMEM((2, 320, 512), BF),
            dma((8,)), dma, dma, dma,
            dma, dma((8,)), dma, dma((8,)), dma, dma((8,)),
            dma, dma((8,)), dma, dma((8,)),
            dma, dma, dma, dma, dma, dma((2, 5)),
            dma, dma((8,)), dma, dma((8,)), dma, dma((8,)),
            dma, dma((8,)), dma((2,)), dma((2,)),
            dma, dma((2, 5)), dma, dma, dma, dma,
        ],
        compiler_params=pltpu.CompilerParams(
            collective_id=0, has_side_effects=True, vmem_limit_bytes=56 << 20
        ),
        cost_estimate=pl.CostEstimate(
            flops=4 * steps * rows * width * 512, bytes_accessed=12 << 20, transcendentals=0
        ),
        name="project_and_reduce",
    )(activations, cotangent, master.T)
    keys, new_master, new_first, new_second = pl.pallas_call(
        update,
        out_shape=(jax.ShapeDtypeStruct((2, 320, 512), BF),) + (jax.ShapeDtypeStruct((64, 256), F32),) * 3,
        in_specs=[vmem] * 5,
        out_specs=(vmem,) * 4,
        name="adam_update",
    )(keys, grad, master.T, first_moment.T, second_moment.T)
    return (keys, new_master.T, new_first.T, new_second.T)


def solution(mesh):
    placed = (
        P(None, ("node", "local"), None),
        P(None, ("node", "local"), None),
        P("node", "local"),
        P("node", "local"),
        P("node", "local"),
    )
    return jax.shard_map(
        per_device,
        mesh=mesh,
        in_specs=placed,
        out_specs=(
            P(None, ("node", "local"), None),
            P("node", "local"),
            P("node", "local"),
            P("node", "local"),
        ),
        check_vma=False,
    )
```

```python
import functools
import math

import jax
import jax.numpy as jnp
from jax import lax
from jax.experimental import pallas as pl
from jax.experimental.pallas import tpu as pltpu
from jax.sharding import PartitionSpec as P

BF = jnp.bfloat16
F32 = jnp.float32
MESH = pl.DeviceIdType.MESH

ORDER = "".join((
    "T0T1G1V0G2P0R0G4H0G3P1T2H1G5G6W0B0H2G7R1H4J0P2R2",
    "H3B1T3J1T4H6H5U2P3J2U1T5H7J4T6B2R3P4R4J3P5P6U3U4",
    "T7J6C0J5B3C1P7S0J7S1S2R5S4R6C2B4S3K0U5B6U6B5S5D0",
    "S6K1D1B7C3R7D2C4K2U7C6S7C5K3C7X0D3Y0D4L0D6D5D7",
))

GROUPS = ((0, 1), (2, 3), (4, 5), (6,))
AHEAD = 2


def device_of(x, y, z, c):
    return ((y // 2) * 16 + z * 2 + c, x * 2 + y % 2)


def kernel(gscale, a_hbm, c_hbm, w_ref, keys_ref, grad_ref,
           a, cb, ct, mb, wt, g, rsib, r1ax, r1bx, r1ay, r1by, r2x, r2y, r3x, r3y, rz, rzb, rz2, rzb2, rz3, rzb3, acc,
           keys, sem_a, sem_c, sem_m, sem_k,
           ag1s, ag1r, ag2s, ag2r, agas, agar, agbs, agbr, agcs, agcr,
           z1s, z1r, z2s, z2r, zrs, zrr,
           sibs, sibr, rsas, rsar, rsbs, rsbr, rs2s, rs2r, rs3s, rs3r,
           szs, szr, sz2s, sz2r, sz3s, sz3r):
    node, local = lax.axis_index("node"), lax.axis_index("local")
    c, z, yh = node % 2, (node // 2) % 8, node // 16
    x, yl = local // 2, local % 2
    y = yh * 2 + yl
    lo, hi = pl.ds(0, 128), pl.ds(128, 128)
    upper, mid, top, low = pl.ds(0, 32), pl.ds(32, 16), pl.ds(0, 48), pl.ds(48, 16)

    def at_x(d):
        return device_of((x + d) % 4, y, z, c)

    def at_y(d):
        return device_of(x, (y + d) % 4, z, c)

    def at_z(d):
        return device_of(x, y, (z + d) % 8, c)

    sibling = device_of(x, y, z, 1 - c)

    def send(src, dst, ss, rs, device):
        return pltpu.make_async_remote_copy(
            src_ref=src, dst_ref=dst, send_sem=ss, recv_sem=rs, device_id=device, device_id_type=MESH
        )

    def arrived(ref, sem):
        pltpu.make_async_copy(ref, ref, sem).wait()

    def pieces(n):
        for per, rest in (
            (16, ()), (8, (0,)), (6, (0, pl.ds(0, 3))), (4, (0, slice(None), 0)),
            (3, (0, pl.ds(0, 3), 0)), (2, (0, 0)), (1, (0, 0, 0)),
        ):
            if n % per == 0 and n // per <= 8:
                return wt.at[(0, pl.ds(0, n // per), *rest)]

    def far_first(i):
        return (z + (4 - (i + 1) // 2 if i % 2 == 1 else 4 + i // 2)) % 8

    def near_first(i):
        return far_first(7 - i)

    barrier = pltpu.get_barrier_semaphore()
    partners = [at_x(d) for d in (1, 2, 3)] + [at_y(d) for d in (1, 2, 3)]
    partners += [at_z(d) for d in range(1, 8)] + [sibling]
    for device in partners:
        pl.semaphore_signal(barrier, inc=1, device_id=device, device_id_type=MESH)

    def load_c(m):
        return pltpu.make_async_copy(c_hbm.at[m], cb.at[pl.ds(320 * m, 320)], sem_c)

    def load_a(zz, h, m):
        block = h * 8 + zz
        return pltpu.make_async_copy(
            a_hbm.at[m, :, pl.ds(pl.multiple_of(block * 512, 512), 512)],
            a.at[block, pl.ds(320 * m, 320)],
            sem_a.at[zz],
        )

    def load_slice(i):
        zz = far_first(i)
        for h in range(2):
            for m in range(2):
                load_a(zz, h, m).start()

    load_m = pltpu.make_async_copy(w_ref, mb, sem_m)
    load_m.start()
    for m in range(2):
        load_c(m).start()
    for i in range(AHEAD):
        load_slice(i)

    def ag1(d):
        piece = wt.at[yh, z, c, x, yl, top]
        return send(piece, piece, ag1s, ag1r.at[d], at_z(d))

    def agz1(d):
        piece = wt.at[yh, z, c, x, yl, low]
        return send(piece, piece, z1s, z1r, at_y(d))

    def agz2(d):
        piece = wt.at[:, z, c, x, :, low]
        return send(piece, piece, z2s, z2r, at_x(d))

    def ring_send(zz, k, up):
        piece = wt.at[:, zz, c, :, :, low]
        if up:
            return send(piece, piece, zrs, zrr.at[0, k], at_z(1))
        return send(piece, piece, zrs, zrr.at[1, k], at_z(7))

    def ring_half(up):
        if up:
            piece = wt.at[0, (z + 5) % 8, c, :, :, low]
            return send(piece, piece, zrs, zrr.at[0, 4], at_z(1))
        piece = wt.at[1, (z + 3) % 8, c, :, :, low]
        return send(piece, piece, zrs, zrr.at[1, 4], at_z(7))

    def ag2(zz, d):
        left = wt.at[yh, zz, c, x, yl, top, lo]
        right = wt.at[yh, zz, c, x, yl, top, hi]
        return (
            send(left, left, ag2s, ag2r.at[zz], at_y(d)),
            send(right, right, ag2s, ag2r.at[zz], at_x(d)),
        )

    def ag_second(i):
        zz = near_first(i)

        @pl.when(i > 0)
        def _():
            ag1((z - zz + 8) % 8).wait_recv()

        for d in (1, 3, 2):
            for copy in ag2(zz, d):
                copy.start()

    def ag_low_second(_):
        arrived(rz3, z1r)
        for d in (1, 3, 2):
            agz2(d).start()

    def ag_low_third(_):
        arrived(rz2, z2r)
        ring_send(z, 1, True).start()
        ring_send(z, 1, False).start()

    def ag_ring(i):
        k = (i + 1) // 2

        @pl.when((i < 7) & (i % 2 == 1))
        def _():
            ring_send(z, k, True).wait_recv()
            pl.when(k < 3)(lambda: ring_send((z - k + 8) % 8, k + 1, True).start())
            pl.when(k == 3)(lambda: ring_half(True).start())

        @pl.when((i > 0) & (i % 2 == 0))
        def _():
            ring_send(z, k, False).wait_recv()
            pl.when(k < 3)(lambda: ring_send((z + k) % 8, k + 1, False).start())
            pl.when(k == 3)(lambda: ring_half(False).start())

        @pl.when(i == 7)
        def _():
            ring_half(True).wait_recv()
            ring_half(False).wait_recv()

    def aga(zz):
        left = wt.at[:, zz, c, x, :, top, lo]
        right = wt.at[yh, zz, c, :, yl, top, hi]
        return (
            send(left, left, agas, agar.at[zz], at_x(1)),
            send(left, left, agas, agar.at[zz], at_x(3)),
            send(right, right, agas, agar.at[zz], at_y(1)),
            send(right, right, agas, agar.at[zz], at_y(3)),
        )

    def agb(zz):
        before, after = (x + 3) % 4, (x + 1) % 4
        below, above = (y + 3) % 4, (y + 1) % 4
        parts = (
            wt.at[0, zz, c, before, :, top, lo],
            wt.at[1, zz, c, after, :, top, lo],
            wt.at[below // 2, zz, c, pl.ds(0, 2), below % 2, top, hi],
            wt.at[above // 2, zz, c, pl.ds(2, 2), above % 2, top, hi],
        )
        to = (at_x(1), at_x(3), at_y(1), at_y(3))
        return tuple(
            send(parts[k], parts[k], agbs, agbr.at[zz], to[k]) for k in range(4)
        )

    def agc(zz):
        part = wt.at[:, zz, c]
        return send(part, part, agcs, agcr.at[zz], sibling)

    def sib(zz, h):
        return send(
            g.at[h, zz, 1 - c], rsib.at[h, zz], sibs, sibr.at[zz], sibling
        )

    def rs_terms(i):
        zz = far_first(i)
        arrived(a.at[pl.ds(0, 2)], sem_a.at[zz])
        if i + AHEAD < 8:
            load_slice(i + AHEAD)
        rows = jnp.concatenate([a[zz], a[8 + zz]], axis=1)
        for half in range(2):
            total = jnp.dot(
                ct[256 * half : 256 * half + 256, :], rows, preferred_element_type=F32
            )
            term = (total * gscale).astype(BF)
            for h in range(2):
                for q in range(2):
                    col = 512 * h + 256 * q
                    g[h, zz, q, 2 * half : 2 * half + 2] = term[:, col : col + 256].reshape(2, 2, 64, 256)
        for h in range(2):
            sib(zz, h).start()

    def add(*terms):
        total = terms[0].astype(F32)
        for term in terms[1:]:
            total = total + term.astype(F32)
        return total.astype(BF)

    def rsa(zz):
        far_x = (x + 2) % 4
        return (
            send(g.at[0, zz, c, far_x, :, upper, lo], r1ax.at[0, zz], rsas, rsar.at[zz], at_x(1)),
            send(g.at[1, zz, c, far_x, :, upper, lo], r1ax.at[1, zz], rsas, rsar.at[zz], at_x(3)),
            send(g.at[1 - yh, zz, c, pl.ds(0, 2), yl, top, hi], r1ay.at[0, zz], rsas,
                 rsar.at[zz], at_y(1)),
            send(g.at[1 - yh, zz, c, pl.ds(2, 2), yl, top, hi], r1ay.at[1, zz], rsas,
                 rsar.at[zz], at_y(3)),
        )

    def rs_pair(i):
        zz = far_first(i)
        arrived(rsib.at[:, zz], sibr.at[zz])
        for h in range(2):

            @pl.loop(0, 4)
            def _(k):
                g[h, zz, c, k] = add(g[h, zz, c, k], rsib[h, zz, k])

        for copy in rsa(zz):
            copy.start()

    def rsb(zz):
        before, after = (x + 3) % 4, (x + 1) % 4
        below, above = (y + 3) % 4, (y + 1) % 4
        return (
            send(g.at[:, zz, c, after, :, upper, lo], r1bx.at[0, zz], rsbs, rsbr.at[zz], at_x(1)),
            send(g.at[:, zz, c, before, :, upper, lo], r1bx.at[1, zz], rsbs, rsbr.at[zz], at_x(3)),
            send(g.at[above // 2, zz, c, :, above % 2, top, hi], r1by.at[0, zz], rsbs,
                 rsbr.at[zz], at_y(1)),
            send(g.at[below // 2, zz, c, :, below % 2, top, hi], r1by.at[1, zz], rsbs,
                 rsbr.at[zz], at_y(3)),
        )

    def rs_pass(i):
        zz = far_first(i)
        before, after = (x + 3) % 4, (x + 1) % 4
        below, above = (y + 3) % 4, (y + 1) % 4
        arrived(r1ax.at[0, pl.ds(0, 5)], rsar.at[zz])
        g[0, zz, c, after, :, upper, lo] = add(g[0, zz, c, after, :, upper, lo], r1ax[0, zz])
        g[1, zz, c, before, :, upper, lo] = add(g[1, zz, c, before, :, upper, lo], r1ax[1, zz])
        for k in range(2):
            g[above // 2, zz, c, k, above % 2, top, hi] = add(
                g[above // 2, zz, c, k, above % 2, top, hi], r1ay[0, zz, k]
            )
            g[below // 2, zz, c, 2 + k, below % 2, top, hi] = add(
                g[below // 2, zz, c, 2 + k, below % 2, top, hi], r1ay[1, zz, k]
            )
        for copy in rsb(zz):
            copy.start()

    def rs2(zz, d):
        to_y, to_x = (y + d) % 4, (x + d) % 4
        return (
            send(g.at[to_y // 2, zz, c, x, to_y % 2, upper, lo], r2x.at[d - 1, zz], rs2s,
                 rs2r.at[zz], at_y(d)),
            send(g.at[yh, zz, c, to_x, yl, top, hi], r2y.at[d - 1, zz], rs2s,
                 rs2r.at[zz], at_x(d)),
        )

    def rs_second(i):
        zz = far_first(i)
        arrived(r1bx.at[0, pl.ds(0, 5)], rsbr.at[zz])
        for h in range(2):
            for k in range(2):
                g[h, zz, c, x, k, upper, lo] = add(
                    g[h, zz, c, x, k, upper, lo], r1bx[0, zz, h, k], r1bx[1, zz, h, k]
                )
        for k in range(4):
            g[yh, zz, c, k, yl, top, hi] = add(g[yh, zz, c, k, yl, top, hi], r1by[0, zz, k], r1by[1, zz, k])
        for d in (1, 3, 2):
            for copy in rs2(zz, d):
                copy.start()

    def rs3(zz, d):
        own, to = g.at[yh, zz, c, x, yl], device_of(x, y, zz, c)
        return (
            send(own.at[upper, lo], r3x.at[d], rs3s.at[0], rs3r.at[0], to),
            send(own.at[top, hi], r3y.at[d], rs3s.at[1], rs3r.at[1], to),
        )

    def rs_third(i):
        zz = far_first(i)
        arrived(r1by.at[0, pl.ds(0, 5), 0], rs2r.at[zz])
        g[yh, zz, c, x, yl, upper, lo] = add(
            g[yh, zz, c, x, yl, upper, lo], r2x[0, zz], r2x[1, zz], r2x[2, zz]
        )
        g[yh, zz, c, x, yl, top, hi] = add(
            g[yh, zz, c, x, yl, top, hi], r2y[0, zz], r2y[1, zz], r2y[2, zz]
        )

        @pl.when(i < 7)
        def _():
            for copy in rs3(zz, (zz - z + 8) % 8):
                copy.start()

    def rz_send(zz, k, up):
        q = 0 if up else 1
        to = at_z(1) if up else at_z(7)
        return (
            send(g.at[:, zz, c, :, :, low], rz.at[q, k], szs, szr.at[q, k], to),
            send(g.at[:, zz, c, :, :, mid, lo], rzb.at[q, k], szs, szr.at[q, k], to),
        )

    def rz_half(up):
        zz = (z + 4) % 8
        q = 0 if up else 1
        to = at_z(1) if up else at_z(7)
        return (
            send(g.at[q, zz, c, :, :, low], rz.at[q, 4, q], szs, szr.at[q, 4], to),
            send(g.at[q, zz, c, :, :, mid, lo], rzb.at[q, 4, q], szs, szr.at[q, 4], to),
        )

    def start(copies):
        for copy in copies:
            copy.start()

    def rz_arrived(up, k):
        arrived(pieces(3 if k == 4 else 6), szr.at[0 if up else 1, k])

    def rz_add(zz, h, q, k):
        for e in range(4):
            g[h, zz, c, e, :, low] = add(g[h, zz, c, e, :, low], rz[q, k, h, e])
            g[h, zz, c, e, :, mid, lo] = add(g[h, zz, c, e, :, mid, lo], rzb[q, k, h, e])

    def rs_ring(i):
        zz = far_first(i)
        k = 4 - (i + 1) // 2
        j = 4 - i // 2

        @pl.when(i == 0)
        def _():
            start(rz_half(True))
            start(rz_half(False))

        @pl.when((i % 2 == 1) & (i < 7))
        def _():
            @pl.when(k == 3)
            def _():
                rz_arrived(True, 4)
                rz_add(zz, 0, 0, 4)

            @pl.when(k < 3)
            def _():
                rz_arrived(True, k + 1)
                rz_add(zz, 0, 0, k + 1)
                rz_add(zz, 1, 0, k + 1)

            start(rz_send(zz, k, True))

        @pl.when((i % 2 == 0) & (i > 0))
        def _():
            @pl.when(j == 3)
            def _():
                rz_arrived(False, 4)
                rz_add(zz, 1, 1, 4)

            @pl.when(j < 3)
            def _():
                rz_arrived(False, j + 1)
                rz_add(zz, 0, 1, j + 1)
                rz_add(zz, 1, 1, j + 1)

            start(rz_send(zz, j, False))

        @pl.when(i == 7)
        def _():
            for q in range(2):
                rz_arrived(q == 0, 1)
                rz_add(z, 0, q, 1)
                rz_add(z, 1, q, 1)
            for d in (1, 3, 2):
                start(rz_second(d))

    def rz_second(d):
        to_x = (x + d) % 4
        return (
            send(g.at[:, z, c, to_x, :, low], rz2.at[d - 1], sz2s, sz2r, at_x(d)),
            send(g.at[:, z, c, to_x, :, mid, lo], rzb2.at[d - 1], sz2s, sz2r, at_x(d)),
        )

    def rz_third(d):
        to_y = (y + d) % 4
        part = g.at[to_y // 2, z, c, x, to_y % 2]
        return (
            send(part.at[low], rz3.at[d - 1], sz3s, sz3r, at_y(d)),
            send(part.at[mid, lo], rzb3.at[d - 1], sz3s, sz3r, at_y(d)),
        )

    def rz_last(_):
        arrived(r1by.at[0, pl.ds(0, 3)], sz2r)
        for h in range(2):
            for k in range(2):
                g[h, z, c, x, k, low] = add(
                    g[h, z, c, x, k, low], rz2[0, h, k], rz2[1, h, k], rz2[2, h, k]
                )
                g[h, z, c, x, k, mid, lo] = add(
                    g[h, z, c, x, k, mid, lo], rzb2[0, h, k], rzb2[1, h, k], rzb2[2, h, k]
                )
        for d in (1, 3, 2):
            start(rz_third(d))

    def project(group):
        slices = [near_first(i) for i in GROUPS[group]]
        for zz in slices:
            agc(zz).wait_recv()
        blocks = [(h, zz) for zz in slices for h in range(2)]
        rows = jnp.concatenate([a[h * 8 + zz] for h, zz in blocks], axis=1)
        piece = jnp.concatenate(
            [wt[h, zz, q].reshape(512, 256) for h, zz in blocks for q in range(2)], axis=1
        )
        total = lax.dot_general(rows, piece, (((1,), (1,)), ((), ())), preferred_element_type=F32)
        acc[...] = acc[...] + total if group > 0 else total

    def project_last(core):
        zz = near_first(7)
        columns = pl.ds(pl.multiple_of(core * 256, 256), 256)
        rows = jnp.concatenate([a[zz, :, columns], a[8 + zz, :, columns]], axis=1)
        piece = jnp.concatenate([wt[h, zz, core].reshape(512, 256) for h in range(2)], axis=1)
        return acc[...] + lax.dot_general(
            rows, piece, (((1,), (1,)), ((), ())), preferred_element_type=F32
        )

    def project_own(_):
        acc[...] = project_last(c)

    def store_keys():
        return pltpu.make_async_copy(keys, keys_ref, sem_k)

    def project_sibling(_):
        agc(near_first(7)).wait_recv()
        keys[...] = project_last(1 - c).astype(BF).reshape(2, 320, 512)
        store_keys().start()

    def ag_a(i):
        zz = near_first(i)
        arrived(r2y.at[:, pl.ds(0, 2)], ag2r.at[zz])
        for copy in aga(zz):
            copy.start()

    def ag_b(i):
        zz = near_first(i)
        arrived(r1ay.at[0], agar.at[zz])
        for copy in agb(zz):
            copy.start()

    def ag_c(i):
        zz = near_first(i)
        arrived(r1ay.at[0, pl.ds(0, 4)], agbr.at[zz])
        agc(zz).start()

    load_m.wait()
    wt[yh, z, c, x, yl] = mb[...].astype(BF)
    pl.semaphore_wait(barrier, len(partners))
    for d in (1, 3, 2):
        agz1(d).start()
    for d in (1, 7, 2, 6, 3, 5, 4):
        ag1(d).start()
    ag_second(0)
    arrived(cb, sem_c)
    ct[...] = cb[...].T

    stages = dict(
        T=rs_terms, P=rs_pair, R=rs_ring, B=rs_pass, C=rs_second, D=rs_third, L=rz_last,
        G=ag_second, V=ag_low_second, W=ag_low_third, H=ag_a, J=ag_b, U=ag_ring, S=ag_c, K=project, X=project_own, Y=project_sibling,
    )
    for letter, digit in zip(ORDER[::2], ORDER[1::2]):
        stages[letter](int(digit))

    def total(rows, columns, terms):
        value = g[yh, z, c, x, yl, rows, columns].astype(F32)
        for term in terms:
            value = value + term.astype(F32)
        grad_ref[rows, columns] = value

    arrived(r3x.at[pl.ds(1, 7)], rs3r.at[0])
    arrived(r3y.at[pl.ds(1, 7)], rs3r.at[1])
    total(upper, lo, [r3x[d] for d in range(1, 8)])
    total(top, hi, [r3y[d] for d in range(1, 8)])
    arrived(r1by.at[0, 0, pl.ds(0, 3)], sz3r)
    total(low, pl.ds(0, 256), [rz3[k] for k in range(3)])
    total(mid, lo, [rzb3[k] for k in range(3)])

    store_keys().wait()

    for ref, sem in (
        (r1by.at[0, pl.ds(0, 7), pl.ds(0, 2)], ag1s), (rz3, z1s), (rz2, z2s), (pieces(28), zrs),
        (pieces(18), ag2s), (pieces(48), agas), (pieces(24), agbs), (rsib, agcs),
        (rsib, sibs), (pieces(20), rsas), (pieces(40), rsbs), (pieces(15), rs2s),
        (r3x.at[pl.ds(1, 7)], rs3s.at[0]), (r3y.at[pl.ds(1, 7)], rs3s.at[1]), (pieces(42), szs),
        (r1by.at[0, pl.ds(0, 3)], sz2s), (r1by.at[0, 0, pl.ds(0, 3)], sz3s),
    ):
        arrived(ref, sem)


def update(keys_ref, grad_ref, master_ref, first_ref, second_ref,
           keys_out, master_out, first_out, second_out):
    keys_out[...] = keys_ref[...]
    grad, master = grad_ref[...], master_ref[...]
    new_first = 0.9 * first_ref[...] + 0.1 * grad
    new_second = 0.95 * second_ref[...] + 0.05 * grad * grad
    mhat = new_first / (1.0 - 0.9**10)
    vhat = new_second / (1.0 - 0.95**10)
    first_out[...] = new_first
    second_out[...] = new_second
    master_out[...] = master - 0.0003 * (mhat / (jnp.sqrt(vhat) + 1e-08) + 0.1 * master)


def per_device(activations, cotangent, master, first_moment, second_moment):
    steps, rows, width = activations.shape
    gscale = 1.0 / math.sqrt(steps * rows * lax.axis_size("node") * lax.axis_size("local"))
    any_spec = pl.BlockSpec(memory_space=pl.ANY)
    vmem = pl.BlockSpec(memory_space=pltpu.VMEM)
    dma = pltpu.SemaphoreType.DMA
    keys, grad = pl.pallas_call(
        functools.partial(kernel, gscale),
        out_shape=(
            jax.ShapeDtypeStruct((2, 320, 512), BF),
            jax.ShapeDtypeStruct((64, 256), F32),
        ),
        in_specs=[any_spec, any_spec, any_spec],
        out_specs=(any_spec, vmem),
        scratch_shapes=[
            pltpu.VMEM((16, 640, 512), BF),
            pltpu.VMEM((640, 512), BF),
            pltpu.VMEM((512, 640), BF),
            pltpu.VMEM((64, 256), F32),
            pltpu.VMEM((2, 8, 2, 4, 2, 64, 256), BF),
            pltpu.VMEM((2, 8, 2, 4, 2, 64, 256), BF),
            pltpu.VMEM((2, 8, 4, 2, 64, 256), BF),
            pltpu.VMEM((2, 8, 2, 32, 128), BF),
            pltpu.VMEM((2, 8, 2, 2, 32, 128), BF),
            pltpu.VMEM((2, 8, 2, 48, 128), BF),
            pltpu.VMEM((2, 8, 4, 48, 128), BF),
            pltpu.VMEM((3, 8, 32, 128), BF),
            pltpu.VMEM((3, 8, 48, 128), BF),
            pltpu.VMEM((8, 32, 128), BF),
            pltpu.VMEM((8, 48, 128), BF),
            pltpu.VMEM((2, 5, 2, 4, 2, 16, 256), BF),
            pltpu.VMEM((2, 5, 2, 4, 2, 16, 128), BF),
            pltpu.VMEM((3, 2, 2, 16, 256), BF),
            pltpu.VMEM((3, 2, 2, 16, 128), BF),
            pltpu.VMEM((3, 16, 256), BF),
            pltpu.VMEM((3, 16, 128), BF),
            pltpu.VMEM((640, 512), F32),
            pltpu.VMEM((2, 320, 512), BF),
            dma((8,)), dma, dma, dma,
            dma, dma((8,)), dma, dma((8,)), dma, dma((8,)),
            dma, dma((8,)), dma, dma((8,)),
            dma, dma, dma, dma, dma, dma((2, 5)),
            dma, dma((8,)), dma, dma((8,)), dma, dma((8,)),
            dma, dma((8,)), dma((2,)), dma((2,)),
            dma, dma((2, 5)), dma, dma, dma, dma,
        ],
        compiler_params=pltpu.CompilerParams(
            collective_id=0, has_side_effects=True, vmem_limit_bytes=56 << 20
        ),
        cost_estimate=pl.CostEstimate(
            flops=4 * steps * rows * width * 512, bytes_accessed=12 << 20, transcendentals=0
        ),
        name="project_and_reduce",
    )(activations, cotangent, master.T)
    keys, new_master, new_first, new_second = pl.pallas_call(
        update,
        out_shape=(jax.ShapeDtypeStruct((2, 320, 512), BF),) + (jax.ShapeDtypeStruct((64, 256), F32),) * 3,
        in_specs=[vmem] * 5,
        out_specs=(vmem,) * 4,
        name="adam_update",
    )(keys, grad, master.T, first_moment.T, second_moment.T)
    return (keys, new_master.T, new_first.T, new_second.T)


def solution(mesh):
    placed = (
        P(None, ("node", "local"), None),
        P(None, ("node", "local"), None),
        P("node", "local"),
        P("node", "local"),
        P("node", "local"),
    )
    return jax.shard_map(
        per_device,
        mesh=mesh,
        in_specs=placed,
        out_specs=(
            P(None, ("node", "local"), None),
            P("node", "local"),
            P("node", "local"),
            P("node", "local"),
        ),
        check_vma=False,
    )
```
